32 devices in a mesh: groups: 2 (over y), ep: 8 (over z, core), rep: 2 (over x).
Axes of the slice: x: 2, y: 2, z: 4, core: 2. Of those that a mesh axis runs over, the one named last changes fastest.
Arguments:
- tokens: bfloat16 [1024, 2048], P(('groups', 'ep')), parts along dimension 0, may hold values from -6 to 6
- choices: int32 [1024, 8], P(('groups', 'ep')), parts along dimension 0, may hold values from 0 to 15, all different within a row; in each aligned block of 64 rows (0 to 63, 64 to 127, ...) at most 64 rows name the same one
- route_weight: float32 [1024, 8], P(('groups', 'ep')), parts along dimension 0, may hold values from 0.05 to 0.3
- gate_proj: bfloat16 [16, 2048, 768], P('ep', None, 'rep'), may hold values from -0.125 to 0.125
- up_proj: bfloat16 [16, 2048, 768], P('ep', None, 'rep'), may hold values from -0.125 to 0.125
- down_proj: bfloat16 [16, 768, 2048], P('ep', 'rep'), may hold values from -0.21875 to 0.21875
Outputs:
- mixed: bfloat16 [1024, 2048], P(('groups', 'ep'), 'rep'), parts along dimension 0
The draws below stay inside these ranges and needn't reach their ends.
There are 2 independent parts, one for each index of `groups`. The reference program is written for one: setup_inputs(seed, part) draws one part's arguments, and reference() takes and returns one part's arrays. A program takes and returns all parts, laid end to end along the dimension named above; an argument that names none is the same for every part. Nothing has to cross between parts.
Inputs may be any that keep to these rules, and one draw needn't show every extreme that they name: `choices`: each row names 8 different experts. In each aligned block of 64 rows no expert is named by more than 64 rows, a bound that some block reaches.
All inputs are finite; a program needn't handle non-finite values.
Results may differ from the reference program's by a relative error of at most 0.0085.
Values may be sent and summed in bfloat16 or wider, within the bound.
A program may use at most 64 MiB of HBM per device.

```python
import math
import jax
import jax.numpy as jnp
import numpy as np
from jax import lax

D = 2048
FF = 768
TOP = 8
TOK_DEV = 64
EXPERTS = 16
TOKENS = 512
CAP = 64
N_EP = 8
N_REP = 2


def shard_levels(rng, extent, cuts, low, top_value):
    loudness = 1.0
    for axis_at, blocks in cuts:
        steps = jax.random.uniform(jax.random.fold_in(jax.random.fold_in(rng, 6), axis_at), (blocks,), jnp.float32, low / len(cuts), top_value / len(cuts))
        loudness = loudness * jnp.repeat(jnp.exp(steps), extent[axis_at] // blocks).reshape((-1,) + (1,) * (len(extent) - 1 - axis_at))
    return loudness


def assign_block(rng, own, number, rows, number_of, top, reach, lean):
    order = jax.random.permutation(rng, number_of)
    crowded, common = load_shares(number_of, rows * top, reach, lean, True), load_shares(number_of, rows * top, reach, lean, False)
    places = jnp.arange(number_of)

    def named(tallies, offset_by):
        used = int((tallies > 0).sum())
        fixed = max(1, used // 4)
        shifted = fixed + (places - fixed + offset_by * (used - fixed)) % max(1, number_of - fixed)
        return jnp.zeros((number_of,), jnp.int32).at[order[jnp.where(places < fixed, places, shifted)]].set(jnp.asarray(tallies, jnp.int32))

    tallies = jnp.where(number % 4 == 0, named(crowded, number // 4), named(common, number - number // 4 - 1))
    mixed = jax.random.permutation(jax.random.fold_in(own, 3), number_of)
    giver, receiver = mixed[0:number_of // 2 * 2:2], mixed[1:number_of // 2 * 2:2]
    slack = jnp.minimum(tallies[giver] - 1, reach - tallies[receiver]) // 2
    slack = jnp.where((giver == order[0]) | (receiver == order[0]) | (tallies[receiver] == 0), 0, jnp.maximum(slack, 0))
    shifted = jax.random.randint(jax.random.fold_in(own, 4), (number_of // 2,), 0, 1 << 20) % (slack + 1)
    tallies = tallies.at[giver].add(-shifted).at[receiver].add(shifted)
    members = jnp.searchsorted(jnp.cumsum(tallies), jnp.arange(rows * top), side="right").astype(jnp.int32)
    grid = members.reshape(top, rows).T
    grid = grid[jax.random.permutation(jax.random.fold_in(own, 1), rows)]
    offset_by = jax.random.randint(jax.random.fold_in(own, 2), (rows, 1), 0, top)
    return jnp.take_along_axis(grid, (jnp.arange(top)[None, :] + offset_by) % top, axis=1)


def load_shares(amount, total, most, slope, full):
    portions = [(1 << 20) // math.isqrt(standing ** slope) + 1 for standing in range(1, amount + 1)]
    largest = most if full else min(most, max(-(-total // amount), total * portions[0] // sum(portions)))
    least = 1 if total - largest >= amount - 1 else 0
    given, spare = [largest] + [least] * (amount - 1), total - largest - least * (amount - 1)
    while spare > 0:
        movable = [i for i in range(1, amount) if given[i] < largest] or [i for i in range(1, amount) if given[i] < most]
        whole, remaining = sum([portions[i] for i in movable]), spare
        for i in movable:
            more = min(most - given[i], max(1, remaining * portions[i] // whole), spare)
            given[i] = given[i] + more
            spare = spare - more
    return np.array(given)


def bell_draw(stream_key, dims, deviation, most, pieces=(), held_as=jnp.bfloat16):
    entries = jax.random.normal(stream_key, dims, jnp.float32) * deviation
    if len(pieces) > 0:
        entries = shard_levels(stream_key, dims, pieces, -0.22, 0.18) * entries
    return jnp.clip(entries, min=-most, max=most).astype(held_as)


def setup_inputs(seed: int = 0, part: int = 0) -> dict:
    key_of = jax.random.split(jax.random.key(seed), 7)
    part_keys = jax.random.split(jax.random.fold_in(key_of[6], part), 7)
    tokens = bell_draw(part_keys[0], (TOKENS, D), 1.0, 6.0, ((0, 8),))
    choices_keys = jax.random.split(jax.random.fold_in(part_keys[1], 1), TOKENS // TOK_DEV)
    choices_turns = jax.random.permutation(jax.random.fold_in(part_keys[1], 3), TOKENS // TOK_DEV)
    choices = jax.vmap(lambda own, number: assign_block(jax.random.fold_in(part_keys[1], 2), own, number, TOK_DEV, EXPERTS, TOP, CAP, 2))(choices_keys, choices_turns).reshape((TOKENS, TOP))
    route_weight = jnp.clip(0.05 + 0.25 * jax.random.uniform(part_keys[2], (TOKENS, TOP), jnp.float32) ** shard_levels(part_keys[2], (TOKENS, TOP), ((0, 8),), -0.2, 0.2), 0.05, 0.3)
    gate_proj = bell_draw(key_of[3], (EXPERTS, D, FF), D ** -0.5, 0.125, ((0, 8), (2, 2)))
    up_proj = bell_draw(key_of[4], (EXPERTS, D, FF), D ** -0.5, 0.125, ((0, 8), (2, 2)))
    down_proj = bell_draw(key_of[5], (EXPERTS, FF, D), FF ** -0.5, 0.21875, ((0, 8), (1, 2)))
    return dict(tokens=tokens, choices=choices, route_weight=route_weight, gate_proj=gate_proj, up_proj=up_proj, down_proj=down_proj)


def reference(tokens, choices, route_weight, gate_proj, up_proj, down_proj):
    flat = choices.reshape(N_EP, TOK_DEV * TOP)
    expert_ids = jnp.arange(EXPERTS, dtype=jnp.int32)
    onehot = (flat[:, :, None] == expert_ids[None, None, :]).astype(jnp.int32)
    before = jnp.cumsum(onehot, axis=1) - onehot
    rank = jnp.sum(before * onehot, axis=2)
    blocks = jnp.arange(N_EP, dtype=jnp.int32)[:, None]
    slot_row = (blocks * CAP + rank).reshape(-1).astype(jnp.int32)
    expert_of = flat.reshape(-1).astype(jnp.int32)
    token_of = (jnp.arange(TOKENS * TOP, dtype=jnp.int32) // TOP).astype(jnp.int32)
    buffer = jnp.zeros((EXPERTS, N_EP * CAP, D), jnp.bfloat16)
    buffer = buffer.at[expert_of, slot_row].set(tokens[token_of])
    quarter = FF // N_REP

    def run_expert(packed):
        rows, gate, upper, down = packed
        total = jnp.zeros((rows.shape[0], D), jnp.float32)
        for part_q in range(N_REP):
            low = part_q * quarter
            high = low + quarter
            gate_val = jnp.dot(rows, gate[:, low:high], preferred_element_type=jnp.float32)
            up_val = jnp.dot(rows, upper[:, low:high], preferred_element_type=jnp.float32)
            hidden = (jax.nn.silu(gate_val) * up_val).astype(jnp.bfloat16)
            partial_q = jnp.dot(hidden, down[low:high, :], preferred_element_type=jnp.float32).astype(jnp.bfloat16)
            partial_q = lax.optimization_barrier(partial_q)
            total = total + partial_q.astype(jnp.float32)
        return total.astype(jnp.bfloat16)

    expert_out = lax.map(run_expert, (buffer, gate_proj, up_proj, down_proj))
    picked = expert_out[expert_of, slot_row].astype(jnp.float32).reshape(TOKENS, TOP, D)
    mixed = jnp.sum(picked * route_weight[:, :, None].astype(jnp.float32), axis=1)
    return mixed.astype(jnp.bfloat16)
```

```python
import functools

import jax
import jax.numpy as jnp
from jax import lax
from jax.experimental import pallas as pl
from jax.experimental.pallas import tpu as pltpu
from jax.sharding import PartitionSpec as P

MESH = pl.DeviceIdType.MESH
BF16 = jnp.bfloat16
F32 = jnp.float32
LANES = 128
N_Z = 4
AG_Z, AG_X, AG_OWN, AG_C, RS_C, RS_X, RS_Z, N_SEM = 0, 4, 8, 9, 17, 21, 25, 29


def partner(z, k):
    return (z, z + 1 - 2 * lax.rem(z, 2), lax.rem(z + 2, 4), 3 - z)[k]


def kernel(
    tokens, choices, route, gate, up, down, out,
    xg, gv, uv, dv, own, c_send, c_recv, x_send, x_recv, z_send, z_recv, acc,
    local_sem, send_sem, recv_sem,
):
    e = lax.axis_index("ep")
    x = lax.axis_index("rep")
    z, c = e // 2, lax.rem(e, 2)
    rows, half = tokens.shape[0], tokens.shape[1] // 2
    pieces = xg.shape[-1]

    weights = []
    for i, (a, b) in enumerate(((gate, gv), (up, uv), (down, dv))):
        for j in range(2):
            weights.append(pltpu.make_async_copy(a.at[j], b.at[j], local_sem.at[2 * i + j]))
    loads = [
        pltpu.make_async_copy(
            tokens.at[:, pl.ds(h * half, half)], xg.at[e, h, :, pl.ds(0, half)], local_sem.at[6 + h]
        )
        for h in range(2)
    ]
    for copy in loads + weights:
        copy.start()

    core_peer, x_peer = {"ep": 2 * z + 1 - c}, {"rep": 1 - x}
    z_peer = [{"ep": 2 * partner(z, k) + c} for k in range(N_Z)]
    barrier = pltpu.get_barrier_semaphore()
    peers = [core_peer, x_peer] + z_peer[1:]
    for peer in peers:
        pl.semaphore_signal(barrier, inc=1, device_id=peer, device_id_type=MESH)

    lane = lax.broadcasted_iota(jnp.int32, (rows, LANES), 1)
    dense = jnp.zeros((rows, LANES), F32)
    for k in range(choices.shape[1]):
        dense = dense + jnp.where(lane == choices[:, k : k + 1], route[:, k : k + 1], 0.0)
    high = dense.astype(BF16)
    xg[e, 0, :, half:pieces] = high
    xg[e, 1, :, half:pieces] = (dense - high.astype(F32)).astype(BF16)
    for copy in loads:
        copy.wait()
    pl.semaphore_wait(barrier, len(peers))

    started = []

    def send(src, dst, slot, peer):
        copy = pltpu.make_async_remote_copy(
            src_ref=src, dst_ref=dst, send_sem=send_sem.at[slot], recv_sem=recv_sem.at[slot],
            device_id=peer, device_id_type=MESH,
        )
        copy.start()
        started.append(copy)

    def arrive(dst, slot, peer):
        pltpu.make_async_remote_copy(
            src_ref=dst, dst_ref=dst, send_sem=send_sem.at[slot], recv_sem=recv_sem.at[slot],
            device_id=peer, device_id_type=MESH,
        ).wait_recv()

    def block(k, core):
        return 2 * partner(z, k) + core

    def gather_z(k):
        piece = xg.at[block(k, c), x]
        arrive(piece, AG_Z + k, z_peer[k])
        send(piece, piece, AG_X + k, x_peer)
        send(piece, piece, AG_C + 2 * k, core_peer)

    def gather_x(k):
        piece = xg.at[block(k, c), 1 - x]
        arrive(piece, AG_X + k, x_peer)
        send(piece, piece, AG_C + 2 * k + 1, core_peer)

    def gather_c(k):
        if k == 0:
            arrive(xg.at[block(0, 1 - c)], AG_OWN, core_peer)
        else:
            arrive(xg.at[block(k, 1 - c), x], AG_C + 2 * k, core_peer)
            arrive(xg.at[block(k, 1 - c), 1 - x], AG_C + 2 * k + 1, core_peer)

    mine = c == 0

    def compute(k):
        at = pl.ds(2 * partner(z, k), 2)
        tok = [xg[at, h, :, 0:half].reshape(2 * rows, half) for h in range(2)]
        w = [xg[at, h, :, half:pieces].reshape(2 * rows, LANES).astype(F32) for h in range(2)]
        w = w[0] + w[1]
        lanes = lax.broadcasted_iota(jnp.int32, w.shape, 1)
        hidden = []
        for j in range(2):
            g, u = (
                jnp.dot(tok[0], ref[j, 0:half], preferred_element_type=F32)
                + jnp.dot(tok[1], ref[j, half : 2 * half], preferred_element_type=F32)
                for ref in (gv, uv)
            )
            weight = jnp.sum(jnp.where(lanes == 2 * e + j, w, 0.0), axis=1, keepdims=True)
            hidden.append((g / (1.0 + jnp.exp(-g)) * u * weight).astype(BF16))
        for h in range(2):
            cols = slice(h * half, (h + 1) * half)
            p = jnp.dot(hidden[0], dv[0, :, cols], preferred_element_type=F32)
            p = p + jnp.dot(hidden[1], dv[1, :, cols], preferred_element_type=F32)
            own[k, h] = jnp.where(mine, p[:rows], p[rows:])
            c_send[k, h] = jnp.where(mine, p[rows:], p[:rows]).astype(BF16)
        send(c_send.at[k], c_recv.at[k], RS_C + k, core_peer)

    def reduce_c(k):
        arrive(c_recv.at[k], RS_C + k, core_peer)
        x_send[k] = (own[k, 1 - x] + c_recv[k, 1 - x].astype(F32)).astype(BF16)
        send(x_send.at[k], x_recv.at[k], RS_X + k, x_peer)

    def reduce_x(k):
        arrive(x_recv.at[k], RS_X + k, x_peer)
        total = own[k, x] + c_recv[k, x].astype(F32) + x_recv[k].astype(F32)
        if k == 0:
            acc[...] = total
        else:
            z_send[k] = total.astype(BF16)
            send(z_send.at[k], z_recv.at[k], RS_Z + k, z_peer[k])

    for k in range(1, N_Z):
        send(xg.at[e, x], xg.at[e, x], AG_Z + k, z_peer[k])
    send(xg.at[e], xg.at[e], AG_OWN, core_peer)

    gather_z(1)
    gather_c(0)
    for copy in weights:
        copy.wait()
    compute(0)
    gather_x(1)
    gather_z(2)
    gather_c(1)
    compute(1)
    reduce_c(0)
    gather_x(2)
    gather_z(3)
    gather_c(2)
    compute(2)
    reduce_c(1)
    reduce_x(0)
    gather_x(3)
    gather_c(3)
    compute(3)
    reduce_c(2)
    reduce_x(1)
    reduce_c(3)
    reduce_x(2)
    reduce_x(3)
    total = acc[...]
    for k in range(1, N_Z):
        arrive(z_recv.at[k], RS_Z + k, z_peer[k])
        total = total + z_recv[k].astype(F32)
    out[...] = total.astype(BF16)
    for copy in started:
        copy.wait_send()


def fused(tokens, choices, route_weight, gate_proj, up_proj, down_proj):
    n_ep = lax.axis_size("ep")
    rows, width = tokens.shape
    half, piece = width // 2, (rows, width // 2)
    anywhere, vmem = pl.BlockSpec(memory_space=pl.ANY), pl.BlockSpec(memory_space=pltpu.VMEM)
    return pl.pallas_call(
        kernel,
        out_shape=jax.ShapeDtypeStruct(piece, BF16),
        in_specs=[anywhere, vmem, vmem, anywhere, anywhere, anywhere],
        out_specs=vmem,
        scratch_shapes=[
            pltpu.VMEM((n_ep, 2, rows, half + LANES), BF16),
            pltpu.VMEM(gate_proj.shape, BF16),
            pltpu.VMEM(up_proj.shape, BF16),
            pltpu.VMEM(down_proj.shape, BF16),
            pltpu.VMEM((N_Z, 2) + piece, F32),
            pltpu.VMEM((N_Z, 2) + piece, BF16),
            pltpu.VMEM((N_Z, 2) + piece, BF16),
            pltpu.VMEM((N_Z,) + piece, BF16),
            pltpu.VMEM((N_Z,) + piece, BF16),
            pltpu.VMEM((N_Z,) + piece, BF16),
            pltpu.VMEM((N_Z,) + piece, BF16),
            pltpu.VMEM(piece, F32),
            pltpu.SemaphoreType.DMA((8,)),
            pltpu.SemaphoreType.DMA((N_SEM,)),
            pltpu.SemaphoreType.DMA((N_SEM,)),
        ],
        compiler_params=pltpu.CompilerParams(
            collective_id=0, has_side_effects=True, vmem_limit_bytes=56 * 2**20
        ),
    )(tokens, choices, route_weight, gate_proj, up_proj, down_proj)


def slotted(tokens, choices, route_weight, gate_proj, up_proj, down_proj):
    n_ep = lax.axis_size("ep")
    n_rep = lax.axis_size("rep")
    exp_dev = gate_proj.shape[0]
    num_experts = exp_dev * n_ep
    tok_rows, width = tokens.shape
    picks = choices.shape[1]
    slot_cap = min(tok_rows, (2 * tok_rows * picks // num_experts + n_rep - 1) // n_rep * n_rep)
    slot_total = num_experts * slot_cap
    flat_choice = choices.reshape(-1)
    onehot = flat_choice[:, None] == jnp.arange(num_experts, dtype=jnp.int32)[None, :]
    order = jnp.arange(flat_choice.shape[0])
    earlier = (order[None, :] < order[:, None]).astype(BF16)
    before = jnp.dot(earlier, onehot.astype(BF16), preferred_element_type=F32)
    rank = jnp.sum(jnp.where(onehot, before, 0.0), axis=1).astype(jnp.int32)
    slot_ids = flat_choice * slot_cap + rank
    all_slots = jnp.arange(slot_total, dtype=jnp.int32)
    select = (slot_ids[:, None] == all_slots[None, :]).reshape(tok_rows, picks, slot_total)
    dispatch = jnp.sum(select.astype(BF16), axis=1)
    combine = jnp.sum(jnp.where(select, route_weight[:, :, None], 0.0), axis=1)
    high = combine.astype(BF16)
    low = (combine - high.astype(F32)).astype(BF16)
    buffer = jnp.einsum("ts,td->sd", dispatch, tokens, preferred_element_type=F32)
    buffer = buffer.astype(BF16).reshape(n_ep, exp_dev, slot_cap, width)
    arrived = lax.all_to_all(buffer, "ep", split_axis=0, concat_axis=0, tiled=True)
    gate_val = jnp.einsum("sjcd,jdh->sjch", arrived, gate_proj, preferred_element_type=F32)
    up_val = jnp.einsum("sjcd,jdh->sjch", arrived, up_proj, preferred_element_type=F32)
    hidden = (jax.nn.silu(gate_val) * up_val).astype(BF16)
    partial_out = jnp.einsum("sjch,jhd->sjcd", hidden, down_proj, preferred_element_type=F32)
    expert_out = lax.psum_scatter(
        partial_out.astype(BF16), "rep", scatter_dimension=3, tiled=True
    )
    returned = lax.all_to_all(expert_out, "ep", split_axis=0, concat_axis=0, tiled=True)
    returned = returned.reshape(slot_total, -1)
    mixed = jnp.dot(high, returned, preferred_element_type=F32)
    mixed = mixed + jnp.dot(low, returned, preferred_element_type=F32)
    return mixed.astype(BF16)


def solution(mesh):
    small = mesh.shape["ep"] == 2 * N_Z and mesh.shape["rep"] == 2
    placed = (
        P(("groups", "ep"), None),
        P(("groups", "ep"), None),
        P(("groups", "ep"), None),
        P("ep", None, "rep"),
        P("ep", None, "rep"),
        P("ep", "rep", None),
    )
    return jax.shard_map(
        fused if small else slotted,
        mesh=mesh,
        in_specs=placed,
        out_specs=P(("groups", "ep"), "rep"),
        check_vma=False,
    )
```

```python
import functools

import jax
import jax.numpy as jnp
from jax import lax
from jax.experimental import pallas as pl
from jax.experimental.pallas import tpu as pltpu
from jax.sharding import PartitionSpec as P

MESH = pl.DeviceIdType.MESH
BF16 = jnp.bfloat16
F32 = jnp.float32
LANES = 128
N_Z = 4
AG_Z, AG_X, AG_OWN, AG_C, RS_C, RS_X, RS_Z, FORWARD, N_SEM = 0, 4, 8, 9, 17, 21, 25, 29, 37


def source(z, k):
    first, last = (3 - z) // 3, z // 3
    return (z, z - 1 + 2 * first, z + 1 + first - 3 * last, 3 * (1 - z // 2))[k]


def kernel(
    tokens, choices, route, gate, up, down, out,
    xg, gv, uv, dv, own, c_send, c_recv, x_send, x_recv, z_send, z_recv, acc,
    local_sem, send_sem, recv_sem,
):
    e = lax.axis_index("ep")
    x = lax.axis_index("rep")
    z, c = e // 2, lax.rem(e, 2)
    rows, half = tokens.shape[0], tokens.shape[1] // 2
    pieces = xg.shape[-1]

    weights = []
    for i, (a, b) in enumerate(((gate, gv), (up, uv), (down, dv))):
        for j in range(2):
            weights.append(pltpu.make_async_copy(a.at[j], b.at[j], local_sem.at[2 * i + j]))
    loads = [
        pltpu.make_async_copy(
            tokens.at[:, pl.ds(h * half, half)], xg.at[e, h, :, pl.ds(0, half)], local_sem.at[6 + h]
        )
        for h in range(2)
    ]
    for copy in loads + weights:
        copy.start()

    core_peer, x_peer = {"ep": 2 * z + 1 - c}, {"rep": 1 - x}
    z_peer = [{"ep": 2 * source(z, k) + c} for k in range(N_Z)]
    right, left = {"ep": 2 * lax.rem(z + 1, N_Z) + c}, {"ep": 2 * lax.rem(z + 3, N_Z) + c}
    barrier = pltpu.get_barrier_semaphore()
    peers = [core_peer, x_peer] + z_peer[1:]
    for peer in peers:
        pl.semaphore_signal(barrier, inc=1, device_id=peer, device_id_type=MESH)

    experts = 2 * lax.axis_size("ep")
    index = lax.broadcasted_iota(jnp.int32, (experts, rows), 0)
    dense = jnp.zeros((experts, rows), F32)
    for k in range(choices.shape[0]):
        dense = dense + jnp.where(index == choices[k : k + 1, :], route[k : k + 1, :], 0.0)
    high = dense.astype(BF16)
    unit = lax.broadcasted_iota(jnp.int32, (experts, LANES), 0)
    unit = (unit == lax.broadcasted_iota(jnp.int32, (experts, LANES), 1)).astype(BF16)
    for h, part in enumerate((high, (dense - high.astype(F32)).astype(BF16))):
        turned = lax.dot_general(
            part, unit, (((0,), (0,)), ((), ())), preferred_element_type=F32
        )
        xg[e, h, :, half:pieces] = turned.astype(BF16)
    for copy in loads:
        copy.wait()
    pl.semaphore_wait(barrier, len(peers))

    started = []

    def remote(src, dst, out_slot, in_slot, peer):
        return pltpu.make_async_remote_copy(
            src_ref=src, dst_ref=dst, send_sem=send_sem.at[out_slot], recv_sem=recv_sem.at[in_slot],
            device_id=peer, device_id_type=MESH,
        )

    def send(src, dst, slot, peer, in_slot=None, when=None):
        copy = remote(src, dst, slot, slot if in_slot is None else in_slot, peer)
        started.append((copy, when))
        if when is None:
            copy.start()
        else:
            pl.when(when)(copy.start)

    def arrive(dst, slot, peer):
        remote(dst, dst, slot, slot, peer).wait_recv()

    def block(k, core):
        return 2 * source(z, k) + core

    def gather_z(k):
        src = source(z, k)
        piece = xg.at[block(k, c), x]
        arrive(piece, AG_Z + src, z_peer[k])
        slot = FORWARD + 2 * k
        if k != 2:
            send(piece, piece, slot, right, AG_Z + src, jnp.logical_and(src < z, z < N_Z - 1))
        if k != 1:
            send(piece, piece, slot + 1, left, AG_Z + src, jnp.logical_and(src > z, z > 0))
        send(piece, piece, AG_X + k, x_peer)
        send(piece, piece, AG_C + 2 * k, core_peer)

    def gather_x(k):
        piece = xg.at[block(k, c), 1 - x]
        arrive(piece, AG_X + k, x_peer)
        send(piece, piece, AG_C + 2 * k + 1, core_peer)

    def gather_c(k):
        if k == 0:
            arrive(xg.at[block(0, 1 - c)], AG_OWN, core_peer)
        else:
            arrive(xg.at[block(k, 1 - c), x], AG_C + 2 * k, core_peer)
            arrive(xg.at[block(k, 1 - c), 1 - x], AG_C + 2 * k + 1, core_peer)

    mine = c == 0

    def compute(k):
        at = pl.ds(2 * source(z, k), 2)
        tok = [xg[at, h, :, 0:half].reshape(2 * rows, half) for h in range(2)]
        w = [xg[at, h, :, half:pieces].reshape(2 * rows, LANES).astype(F32) for h in range(2)]
        w = w[0] + w[1]
        lanes = lax.broadcasted_iota(jnp.int32, w.shape, 1)
        hidden = []
        for j in range(2):
            g, u = (
                jnp.dot(tok[0], ref[j, 0:half], preferred_element_type=F32)
                + jnp.dot(tok[1], ref[j, half : 2 * half], preferred_element_type=F32)
                for ref in (gv, uv)
            )
            weight = jnp.sum(jnp.where(lanes == 2 * e + j, w, 0.0), axis=1, keepdims=True)
            hidden.append((g / (1.0 + jnp.exp(-g)) * u * weight).astype(BF16))
        for h in range(2):
            cols = slice(h * half, (h + 1) * half)
            p = jnp.dot(hidden[0], dv[0, :, cols], preferred_element_type=F32)
            p = p + jnp.dot(hidden[1], dv[1, :, cols], preferred_element_type=F32)
            own[k, h] = jnp.where(mine, p[:rows], p[rows:])
            c_send[k, h] = jnp.where(mine, p[rows:], p[:rows]).astype(BF16)
        send(c_send.at[k], c_recv.at[k], RS_C + k, core_peer)

    def reduce_c(k):
        arrive(c_recv.at[k], RS_C + k, core_peer)
        x_send[k] = (own[k, 1 - x] + c_recv[k, 1 - x].astype(F32)).astype(BF16)
        send(x_send.at[k], x_recv.at[k], RS_X + k, x_peer)

    def reduce_x(k):
        arrive(x_recv.at[k], RS_X + k, x_peer)
        total = own[k, x] + c_recv[k, x].astype(F32) + x_recv[k].astype(F32)
        if k == 0:
            acc[...] = total
        else:
            z_send[k] = total.astype(BF16)
            send(z_send.at[k], z_recv.at[z], RS_Z + k, z_peer[k], RS_Z + z)

    send(xg.at[e, x], xg.at[e, x], FORWARD, right, AG_Z + z, z < N_Z - 1)
    send(xg.at[e, x], xg.at[e, x], FORWARD + 1, left, AG_Z + z, z > 0)
    send(xg.at[e], xg.at[e], AG_OWN, core_peer)

    gather_z(1)
    gather_c(0)
    for copy in weights:
        copy.wait()
    compute(0)
    gather_z(2)
    gather_x(1)
    gather_z(3)
    reduce_c(0)
    gather_c(1)
    compute(1)
    gather_x(2)
    reduce_c(1)
    gather_c(2)
    compute(2)
    gather_x(3)
    reduce_c(2)
    reduce_x(0)
    gather_c(3)
    compute(3)
    reduce_x(1)
    reduce_c(3)
    reduce_x(2)
    reduce_x(3)
    total = acc[...]
    for k in range(1, N_Z):
        src = source(z, k)
        arrive(z_recv.at[src], RS_Z + src, z_peer[k])
        total = total + z_recv[src].astype(F32)
    out[...] = total.astype(BF16)
    for copy, when in started:
        if when is None:
            copy.wait_send()
        else:
            pl.when(when)(copy.wait_send)


def fused(tokens, choices, route_weight, gate_proj, up_proj, down_proj):
    n_ep = lax.axis_size("ep")
    rows, width = tokens.shape
    half, piece = width // 2, (rows, width // 2)
    anywhere, vmem = pl.BlockSpec(memory_space=pl.ANY), pl.BlockSpec(memory_space=pltpu.VMEM)
    return pl.pallas_call(
        kernel,
        out_shape=jax.ShapeDtypeStruct(piece, BF16),
        in_specs=[anywhere, vmem, vmem, anywhere, anywhere, anywhere],
        out_specs=vmem,
        scratch_shapes=[
            pltpu.VMEM((n_ep, 2, rows, half + LANES), BF16),
            pltpu.VMEM(gate_proj.shape, BF16),
            pltpu.VMEM(up_proj.shape, BF16),
            pltpu.VMEM(down_proj.shape, BF16),
            pltpu.VMEM((N_Z, 2) + piece, F32),
            pltpu.VMEM((N_Z, 2) + piece, BF16),
            pltpu.VMEM((N_Z, 2) + piece, BF16),
            pltpu.VMEM((N_Z,) + piece, BF16),
            pltpu.VMEM((N_Z,) + piece, BF16),
            pltpu.VMEM((N_Z,) + piece, BF16),
            pltpu.VMEM((N_Z,) + piece, BF16),
            pltpu.VMEM(piece, F32),
            pltpu.SemaphoreType.DMA((8,)),
            pltpu.SemaphoreType.DMA((N_SEM,)),
            pltpu.SemaphoreType.DMA((N_SEM,)),
        ],
        compiler_params=pltpu.CompilerParams(
            collective_id=0, has_side_effects=True, vmem_limit_bytes=56 * 2**20
        ),
    )(tokens, choices.T, route_weight.T, gate_proj, up_proj, down_proj)


def slotted(tokens, choices, route_weight, gate_proj, up_proj, down_proj):
    n_ep = lax.axis_size("ep")
    n_rep = lax.axis_size("rep")
    exp_dev = gate_proj.shape[0]
    num_experts = exp_dev * n_ep
    tok_rows, width = tokens.shape
    picks = choices.shape[1]
    slot_cap = min(tok_rows, (2 * tok_rows * picks // num_experts + n_rep - 1) // n_rep * n_rep)
    slot_total = num_experts * slot_cap
    flat_choice = choices.reshape(-1)
    onehot = flat_choice[:, None] == jnp.arange(num_experts, dtype=jnp.int32)[None, :]
    order = jnp.arange(flat_choice.shape[0])
    earlier = (order[None, :] < order[:, None]).astype(BF16)
    before = jnp.dot(earlier, onehot.astype(BF16), preferred_element_type=F32)
    rank = jnp.sum(jnp.where(onehot, before, 0.0), axis=1).astype(jnp.int32)
    slot_ids = flat_choice * slot_cap + rank
    all_slots = jnp.arange(slot_total, dtype=jnp.int32)
    select = (slot_ids[:, None] == all_slots[None, :]).reshape(tok_rows, picks, slot_total)
    dispatch = jnp.sum(select.astype(BF16), axis=1)
    combine = jnp.sum(jnp.where(select, route_weight[:, :, None], 0.0), axis=1)
    high = combine.astype(BF16)
    low = (combine - high.astype(F32)).astype(BF16)
    buffer = jnp.einsum("ts,td->sd", dispatch, tokens, preferred_element_type=F32)
    buffer = buffer.astype(BF16).reshape(n_ep, exp_dev, slot_cap, width)
    arrived = lax.all_to_all(buffer, "ep", split_axis=0, concat_axis=0, tiled=True)
    gate_val = jnp.einsum("sjcd,jdh->sjch", arrived, gate_proj, preferred_element_type=F32)
    up_val = jnp.einsum("sjcd,jdh->sjch", arrived, up_proj, preferred_element_type=F32)
    hidden = (jax.nn.silu(gate_val) * up_val).astype(BF16)
    partial_out = jnp.einsum("sjch,jhd->sjcd", hidden, down_proj, preferred_element_type=F32)
    expert_out = lax.psum_scatter(
        partial_out.astype(BF16), "rep", scatter_dimension=3, tiled=True
    )
    returned = lax.all_to_all(expert_out, "ep", split_axis=0, concat_axis=0, tiled=True)
    returned = returned.reshape(slot_total, -1)
    mixed = jnp.dot(high, returned, preferred_element_type=F32)
    mixed = mixed + jnp.dot(low, returned, preferred_element_type=F32)
    return mixed.astype(BF16)


def solution(mesh):
    small = mesh.shape["ep"] == 2 * N_Z and mesh.shape["rep"] == 2
    placed = (
        P(("groups", "ep"), None),
        P(("groups", "ep"), None),
        P(("groups", "ep"), None),
        P("ep", None, "rep"),
        P("ep", None, "rep"),
        P("ep", "rep", None),
    )
    return jax.shard_map(
        fused if small else slotted,
        mesh=mesh,
        in_specs=placed,
        out_specs=P(("groups", "ep"), "rep"),
        check_vma=False,
    )
```

```python
import functools

import jax
import jax.numpy as jnp
from jax import lax
from jax.experimental import pallas as pl
from jax.experimental.pallas import tpu as pltpu
from jax.sharding import PartitionSpec as P

MESH = pl.DeviceIdType.MESH
BF16 = jnp.bfloat16
F32 = jnp.float32
LANES = 128
N_Z = 4
PARTS = 2
AG_Z, AG_X, AG_OWN, AG_C, RS_C, RS_X, RS_Z, FORWARD, N_SEM = 0, 4, 8, 9, 17, 21, 25, 29, 37


def source(z, k):
    first, last = (3 - z) // 3, z // 3
    return (z, z - 1 + 2 * first, z + 1 + first - 3 * last, 3 * (1 - z // 2))[k]


def kernel(
    tokens, choices, route, gate, up, down, out,
    xg, gv, uv, dv, own, c_send, c_recv, x_send, x_recv, z_send, z_recv, acc,
    local_sem, send_sem, recv_sem,
):
    e = lax.axis_index("ep")
    x = lax.axis_index("rep")
    z, c = e // 2, lax.rem(e, 2)
    rows, half = tokens.shape[0], tokens.shape[1] // 2
    pieces = xg.shape[-1]

    weights = []
    for i, (a, b) in enumerate(((gate, gv), (up, uv), (down, dv))):
        for j in range(2):
            weights.append(pltpu.make_async_copy(a.at[j], b.at[j], local_sem.at[2 * i + j]))
    loads = [
        pltpu.make_async_copy(
            tokens.at[:, pl.ds(h * half, half)], xg.at[e, h, :, pl.ds(0, half)], local_sem.at[6 + h]
        )
        for h in range(2)
    ]
    for copy in loads + weights:
        copy.start()

    core_peer, x_peer = {"ep": 2 * z + 1 - c}, {"rep": 1 - x}
    z_peer = [{"ep": 2 * source(z, k) + c} for k in range(N_Z)]
    right, left = {"ep": 2 * lax.rem(z + 1, N_Z) + c}, {"ep": 2 * lax.rem(z + 3, N_Z) + c}
    barrier = pltpu.get_barrier_semaphore()
    peers = [core_peer, x_peer] + z_peer[1:]
    for peer in peers:
        pl.semaphore_signal(barrier, inc=1, device_id=peer, device_id_type=MESH)

    experts = 2 * lax.axis_size("ep")
    index = lax.broadcasted_iota(jnp.int32, (experts, rows), 0)
    dense = jnp.zeros((experts, rows), F32)
    for k in range(choices.shape[0]):
        dense = dense + jnp.where(index == choices[k : k + 1, :], route[k : k + 1, :], 0.0)
    high = dense.astype(BF16)
    unit = lax.broadcasted_iota(jnp.int32, (experts, LANES), 0)
    unit = (unit == lax.broadcasted_iota(jnp.int32, (experts, LANES), 1)).astype(BF16)
    for h, part in enumerate((high, (dense - high.astype(F32)).astype(BF16))):
        turned = lax.dot_general(
            part, unit, (((0,), (0,)), ((), ())), preferred_element_type=F32
        )
        xg[e, h, :, half:pieces] = turned.astype(BF16)
    for copy in loads:
        copy.wait()
    pl.semaphore_wait(barrier, len(peers))

    started = []

    def remote(src, dst, out_slot, in_slot, peer, r):
        return pltpu.make_async_remote_copy(
            src_ref=src, dst_ref=dst, send_sem=send_sem.at[out_slot, r], recv_sem=recv_sem.at[in_slot, r],
            device_id=peer, device_id_type=MESH,
        )

    def send(src, dst, slot, peer, in_slot=None, when=None, r=0):
        copy = remote(src, dst, slot, slot if in_slot is None else in_slot, peer, r)
        started.append((copy, when))
        if when is None:
            copy.start()
        else:
            pl.when(when)(copy.start)

    def arrive(dst, slot, peer, r=0):
        remote(dst, dst, slot, slot, peer, r).wait_recv()

    def cut(r):
        return pl.ds(r * (rows // PARTS), rows // PARTS)

    def block(k, core):
        return 2 * source(z, k) + core

    def gather_z(k):
        src, slot = source(z, k), FORWARD + 2 * k
        for r in range(PARTS):
            piece = xg.at[block(k, c), x, cut(r)]
            arrive(piece, AG_Z + src, z_peer[k], r)
            if k != 2:
                on = jnp.logical_and(src < z, z < N_Z - 1)
                send(piece, piece, slot, right, AG_Z + src, on, r)
            if k != 1:
                on = jnp.logical_and(src > z, z > 0)
                send(piece, piece, slot + 1, left, AG_Z + src, on, r)
            send(piece, piece, AG_X + k, x_peer, r=r)
            send(piece, piece, AG_C + 2 * k, core_peer, r=r)

    def gather_x(k):
        for r in range(PARTS):
            piece = xg.at[block(k, c), 1 - x, cut(r)]
            arrive(piece, AG_X + k, x_peer, r)
            send(piece, piece, AG_C + 2 * k + 1, core_peer, r=r)

    def gather_c(k):
        if k == 0:
            arrive(xg.at[block(0, 1 - c)], AG_OWN, core_peer)
            return
        for r in range(PARTS):
            arrive(xg.at[block(k, 1 - c), x, cut(r)], AG_C + 2 * k, core_peer, r)
            arrive(xg.at[block(k, 1 - c), 1 - x, cut(r)], AG_C + 2 * k + 1, core_peer, r)

    mine = c == 0

    def compute(k):
        at = pl.ds(2 * source(z, k), 2)
        tok = [xg[at, h, :, 0:half].reshape(2 * rows, half) for h in range(2)]
        w = [xg[at, h, :, half:pieces].reshape(2 * rows, LANES).astype(F32) for h in range(2)]
        w = w[0] + w[1]
        lanes = lax.broadcasted_iota(jnp.int32, w.shape, 1)
        hidden = []
        for j in range(2):
            g, u = (
                jnp.dot(tok[0], ref[j, 0:half], preferred_element_type=F32)
                + jnp.dot(tok[1], ref[j, half : 2 * half], preferred_element_type=F32)
                for ref in (gv, uv)
            )
            weight = jnp.sum(jnp.where(lanes == 2 * e + j, w, 0.0), axis=1, keepdims=True)
            hidden.append((g / (1.0 + jnp.exp(-g)) * u * weight).astype(BF16))
        for h in range(2):
            cols = slice(h * half, (h + 1) * half)
            p = jnp.dot(hidden[0], dv[0, :, cols], preferred_element_type=F32)
            p = p + jnp.dot(hidden[1], dv[1, :, cols], preferred_element_type=F32)
            own[k, h] = jnp.where(mine, p[:rows], p[rows:])
            c_send[k, h] = jnp.where(mine, p[rows:], p[:rows]).astype(BF16)
        send(c_send.at[k], c_recv.at[k], RS_C + k, core_peer)

    def reduce_c(k):
        arrive(c_recv.at[k], RS_C + k, core_peer)
        for r in range(PARTS):
            at = cut(r)
            x_send[k, at] = (own[k, 1 - x, at] + c_recv[k, 1 - x, at].astype(F32)).astype(BF16)
            send(x_send.at[k, at], x_recv.at[k, at], RS_X + k, x_peer, r=r)

    def reduce_x(k):
        for r in range(PARTS):
            at = cut(r)
            arrive(x_recv.at[k, at], RS_X + k, x_peer, r)
            total = own[k, x, at] + c_recv[k, x, at].astype(F32) + x_recv[k, at].astype(F32)
            if k == 0:
                acc[at] = total
            else:
                z_send[k, at] = total.astype(BF16)
                send(z_send.at[k, at], z_recv.at[z, at], RS_Z + k, z_peer[k], RS_Z + z, r=r)

    for r in range(PARTS):
        piece = xg.at[e, x, cut(r)]
        send(piece, piece, FORWARD, right, AG_Z + z, z < N_Z - 1, r)
        send(piece, piece, FORWARD + 1, left, AG_Z + z, z > 0, r)
    send(xg.at[e], xg.at[e], AG_OWN, core_peer)

    gather_z(1)
    gather_c(0)
    for copy in weights:
        copy.wait()
    compute(0)
    gather_z(2)
    gather_x(1)
    gather_z(3)
    reduce_c(0)
    gather_c(1)
    compute(1)
    gather_x(2)
    reduce_c(1)
    gather_c(2)
    compute(2)
    gather_x(3)
    reduce_c(2)
    reduce_x(0)
    gather_c(3)
    compute(3)
    reduce_x(1)
    reduce_c(3)
    reduce_x(2)
    reduce_x(3)
    for r in range(PARTS):
        at = cut(r)
        total = acc[at]
        for k in range(1, N_Z):
            src = source(z, k)
            arrive(z_recv.at[src, at], RS_Z + src, z_peer[k], r)
            total = total + z_recv[src, at].astype(F32)
        out[at] = total.astype(BF16)
    for copy, when in started:
        if when is None:
            copy.wait_send()
        else:
            pl.when(when)(copy.wait_send)


def fused(tokens, choices, route_weight, gate_proj, up_proj, down_proj):
    n_ep = lax.axis_size("ep")
    rows, width = tokens.shape
    half, piece = width // 2, (rows, width // 2)
    anywhere, vmem = pl.BlockSpec(memory_space=pl.ANY), pl.BlockSpec(memory_space=pltpu.VMEM)
    return pl.pallas_call(
        kernel,
        out_shape=jax.ShapeDtypeStruct(piece, BF16),
        in_specs=[anywhere, vmem, vmem, anywhere, anywhere, anywhere],
        out_specs=vmem,
        scratch_shapes=[
            pltpu.VMEM((n_ep, 2, rows, half + LANES), BF16),
            pltpu.VMEM(gate_proj.shape, BF16),
            pltpu.VMEM(up_proj.shape, BF16),
            pltpu.VMEM(down_proj.shape, BF16),
            pltpu.VMEM((N_Z, 2) + piece, F32),
            pltpu.VMEM((N_Z, 2) + piece, BF16),
            pltpu.VMEM((N_Z, 2) + piece, BF16),
            pltpu.VMEM((N_Z,) + piece, BF16),
            pltpu.VMEM((N_Z,) + piece, BF16),
            pltpu.VMEM((N_Z,) + piece, BF16),
            pltpu.VMEM((N_Z,) + piece, BF16),
            pltpu.VMEM(piece, F32),
            pltpu.SemaphoreType.DMA((8,)),
            pltpu.SemaphoreType.DMA((N_SEM, PARTS)),
            pltpu.SemaphoreType.DMA((N_SEM, PARTS)),
        ],
        compiler_params=pltpu.CompilerParams(
            collective_id=0, has_side_effects=True, vmem_limit_bytes=56 * 2**20
        ),
    )(tokens, choices.T, route_weight.T, gate_proj, up_proj, down_proj)


def slotted(tokens, choices, route_weight, gate_proj, up_proj, down_proj):
    n_ep = lax.axis_size("ep")
    n_rep = lax.axis_size("rep")
    exp_dev = gate_proj.shape[0]
    num_experts = exp_dev * n_ep
    tok_rows, width = tokens.shape
    picks = choices.shape[1]
    slot_cap = min(tok_rows, (2 * tok_rows * picks // num_experts + n_rep - 1) // n_rep * n_rep)
    slot_total = num_experts * slot_cap
    flat_choice = choices.reshape(-1)
    onehot = flat_choice[:, None] == jnp.arange(num_experts, dtype=jnp.int32)[None, :]
    order = jnp.arange(flat_choice.shape[0])
    earlier = (order[None, :] < order[:, None]).astype(BF16)
    before = jnp.dot(earlier, onehot.astype(BF16), preferred_element_type=F32)
    rank = jnp.sum(jnp.where(onehot, before, 0.0), axis=1).astype(jnp.int32)
    slot_ids = flat_choice * slot_cap + rank
    all_slots = jnp.arange(slot_total, dtype=jnp.int32)
    select = (slot_ids[:, None] == all_slots[None, :]).reshape(tok_rows, picks, slot_total)
    dispatch = jnp.sum(select.astype(BF16), axis=1)
    combine = jnp.sum(jnp.where(select, route_weight[:, :, None], 0.0), axis=1)
    high = combine.astype(BF16)
    low = (combine - high.astype(F32)).astype(BF16)
    buffer = jnp.einsum("ts,td->sd", dispatch, tokens, preferred_element_type=F32)
    buffer = buffer.astype(BF16).reshape(n_ep, exp_dev, slot_cap, width)
    arrived = lax.all_to_all(buffer, "ep", split_axis=0, concat_axis=0, tiled=True)
    gate_val = jnp.einsum("sjcd,jdh->sjch", arrived, gate_proj, preferred_element_type=F32)
    up_val = jnp.einsum("sjcd,jdh->sjch", arrived, up_proj, preferred_element_type=F32)
    hidden = (jax.nn.silu(gate_val) * up_val).astype(BF16)
    partial_out = jnp.einsum("sjch,jhd->sjcd", hidden, down_proj, preferred_element_type=F32)
    expert_out = lax.psum_scatter(
        partial_out.astype(BF16), "rep", scatter_dimension=3, tiled=True
    )
    returned = lax.all_to_all(expert_out, "ep", split_axis=0, concat_axis=0, tiled=True)
    returned = returned.reshape(slot_total, -1)
    mixed = jnp.dot(high, returned, preferred_element_type=F32)
    mixed = mixed + jnp.dot(low, returned, preferred_element_type=F32)
    return mixed.astype(BF16)


def solution(mesh):
    small = mesh.shape["ep"] == 2 * N_Z and mesh.shape["rep"] == 2
    placed = (
        P(("groups", "ep"), None),
        P(("groups", "ep"), None),
        P(("groups", "ep"), None),
        P("ep", None, "rep"),
        P("ep", None, "rep"),
        P("ep", "rep", None),
    )
    return jax.shard_map(
        fused if small else slotted,
        mesh=mesh,
        in_specs=placed,
        out_specs=P(("groups", "ep"), "rep"),
        check_vma=False,
    )
```
